32 devices in a mesh: parts: 2 (over y), node: 4 (over z), local: 4 (over x, core).
Axes of the slice: x: 2, y: 2, z: 4, core: 2. Of those that a mesh axis runs over, the one named last changes fastest.
Arguments:
- tokens: bfloat16 [256, 7168], P(('parts', 'node', 'local')), parts along dimension 0, may hold values from -6 to 6
- expert_ids: int32 [256, 8], P(('parts', 'node', 'local')), parts along dimension 0, may hold values from 0 to 15, as said below
- gate_weights: bfloat16 [256, 8], P(('parts', 'node', 'local')), parts along dimension 0, may hold values from 0.099609375 to 1
- w_gate_up: bfloat16 [16, 7168, 2048], P(('node', 'local')), may hold values from -0.0625 to 0.0625
- gate_up_scales: float32 [16, 56, 16], P(('node', 'local')), may hold values from 0.5 to 2
- w_down: bfloat16 [16, 1024, 7168], P(('node', 'local')), may hold values from -0.1875 to 0.1875
- down_scales: float32 [16, 8, 56], P(('node', 'local')), may hold values from 0.5 to 2
Outputs:
- combined: bfloat16 [256, 7168], P(('parts', 'node', 'local')), parts along dimension 0
The draws below stay inside these ranges and needn't reach their ends.
There are 2 independent parts, one for each index of `parts`. The reference program is written for one: setup_inputs(seed, part) draws one part's arguments, and reference() takes and returns one part's arrays. A program takes and returns all parts, laid end to end along the dimension named above; an argument that names none is the same for every part. Nothing has to cross between parts.
Inputs may be any that keep to these rules, and one draw needn't show every extreme that they name: `expert_ids`: each row names 8 different experts, 2 in each of 4 different node groups; expert e belongs to node group e // 4. Among the 8 rows of one device no expert is named by more than 4 rows, and one expert is named by exactly 4 rows of every device.
All inputs are finite; a program needn't handle non-finite values.
Results may differ from the reference program's by a relative error of at most 0.011.
Values may be sent and summed in bfloat16 or wider, within the bound.
No kernel may reach another device: no remote copies, remote signals or barrier semaphores. Data moves between devices by JAX's collectives and lax.ppermute only.
A program may use at most 128 MiB of HBM per device.

```python
import math
import jax
import jax.numpy as jnp
from jax import lax

D = 7168
FFW = 1024
TOPK = 8
GROUP_LIMIT = 4
EXP_GROUP = 4
EXPERTS = 16
SHARD = 1
FFW_DEV = 1024
ROWS = 128
ROUND = 2
CAP = 4
N_NODE = 4
N_LOCAL = 4


def draw_expert_ids(key, part):
    key = jax.random.fold_in(key, 7)
    key_hot, key_group, key_order = jax.random.split(key, 3)
    group_count = N_NODE
    member_count = EXP_GROUP
    per_group = TOPK // GROUP_LIMIT
    round_count = ROWS // ROUND
    hot_expert = jax.random.randint(key_hot, (), 0, group_count * member_count)
    hot_group = hot_expert // member_count
    hot_member = hot_expert % member_count
    group_score = jax.random.randint(key_group, (round_count, ROUND, group_count), 0, 1 << 20) * group_count + jnp.arange(group_count)
    leader = (jnp.arange(ROUND) == 0)[None, :, None] & (jnp.arange(group_count) == hot_group)[None, None, :]
    group_score = jnp.where(leader, -1, group_score)
    picked = jnp.argsort(group_score, axis=-1)[:, :, :GROUP_LIMIT]
    chosen = jnp.sum((picked[..., None] == jnp.arange(group_count)).astype(jnp.int32), axis=2)
    earlier = jnp.cumsum(chosen, axis=1) - chosen
    order_score = jax.random.randint(key_order, (round_count, group_count, member_count), 0, 1 << 20) * member_count + jnp.arange(member_count)
    first_slot = (jnp.arange(group_count) == hot_group)[None, :, None] & (jnp.arange(member_count) == hot_member)[None, None, :]
    order_score = jnp.where(first_slot, -1, order_score)
    shuffled = jnp.argsort(order_score, axis=-1)
    shuffled = jnp.broadcast_to(shuffled[:, None, :, :], (round_count, ROUND, group_count, member_count))
    user_rank = jnp.take_along_axis(earlier, picked, axis=2)
    slot_index = user_rank[..., None] * per_group + jnp.arange(per_group)
    group_lists = jnp.take_along_axis(shuffled, picked[..., None], axis=2)
    member_ids = jnp.take_along_axis(group_lists, slot_index, axis=3)
    expert_list = picked[..., None] * member_count + member_ids
    return expert_list.reshape(ROWS, TOPK).astype(jnp.int32)


def block_levels(key, dims, shards, low, high):
    gain, own = 1.0, jax.random.fold_in(key, 6)
    for position, blocks in shards:
        draws = jnp.exp(jax.random.uniform(jax.random.fold_in(own, position), (blocks,), jnp.float32, low / len(shards), high / len(shards)))
        gain = gain * jnp.repeat(draws, dims[position] // blocks).reshape([-1 if axis == position else 1 for axis in range(len(dims))])
    return gain


def bell_draw(rng, dims, deviation, limit, pieces=(), kind=jnp.bfloat16):
    drawn = deviation * jax.random.normal(rng, dims, jnp.float32)
    if pieces:
        drawn = drawn * block_levels(rng, dims, pieces, -0.22, 0.18)
    return jnp.clip(drawn, -limit, limit).astype(kind)


def setup_inputs(seed: int = 0, part: int = 0) -> dict:
    arg_keys = jax.random.split(jax.random.key(seed), 8)
    part_splits = jax.random.split(jax.random.fold_in(arg_keys[7], part), 8)
    tokens = bell_draw(part_splits[0], (ROWS, D), 1.0, 6.0, ((0, 16),))
    expert_ids = draw_expert_ids(jax.random.fold_in(jax.random.fold_in(arg_keys[7], part), 71), part)
    gate_weights = jnp.clip(jnp.exp(math.log(1.0) - 2.306499 * jax.random.uniform(part_splits[2], (ROWS, TOPK), jnp.float32) ** block_levels(part_splits[2], (ROWS, TOPK), ((0, 16),), -0.2, 0.2)), 0.099609375, 1.0).astype(jnp.bfloat16)
    w_gate_up = bell_draw(arg_keys[3], (EXPERTS * SHARD, D, 2 * FFW_DEV), D ** -0.5, 0.0625, ((0, 16),))
    gate_up_scales = jnp.clip(jnp.exp(math.log(2.0) - 1.3862944 * jax.random.uniform(arg_keys[4], (EXPERTS * SHARD, D // 128, 2 * FFW_DEV // 128), jnp.float32) ** block_levels(arg_keys[4], (EXPERTS * SHARD, D // 128, 2 * FFW_DEV // 128), ((0, 16),), -0.2, 0.2)), 0.5, 2.0)
    w_down = bell_draw(arg_keys[5], (EXPERTS * SHARD, FFW_DEV, D), FFW ** -0.5, 0.1875, ((0, 16),))
    down_scales = jnp.clip(jnp.exp(math.log(2.0) - 1.3862944 * jax.random.uniform(arg_keys[6], (EXPERTS * SHARD, FFW_DEV // 128, D // 128), jnp.float32) ** block_levels(arg_keys[6], (EXPERTS * SHARD, FFW_DEV // 128, D // 128), ((0, 16),), -0.2, 0.2)), 0.5, 2.0)
    return dict(tokens=tokens, expert_ids=expert_ids, gate_weights=gate_weights, w_gate_up=w_gate_up, gate_up_scales=gate_up_scales, w_down=w_down, down_scales=down_scales)


def block_project(operand, weights, scales):
    row_total, inner = operand.shape
    out_width = weights.shape[1]
    blocked = operand.astype(jnp.float32).reshape(row_total, inner // 128, 128)
    weight_blocks = weights.astype(jnp.float32).reshape(inner // 128, 128, out_width)
    products = jnp.einsum("mkc,kcn->mkn", blocked, weight_blocks, precision=lax.Precision.HIGHEST)
    column_scale = jnp.repeat(scales.astype(jnp.float32), 128, axis=1)
    return jnp.sum(products * column_scale[None], axis=1)


def expert_apply(operand, gate_up, gate_up_scale, down, down_scale):
    half_width = down.shape[0]
    hidden_pair = block_project(operand, gate_up, gate_up_scale)
    activation = (jax.nn.silu(hidden_pair[:, :half_width]) * hidden_pair[:, half_width:]).astype(jnp.bfloat16)
    return block_project(activation, down, down_scale).astype(jnp.bfloat16)


def reference(tokens, expert_ids, gate_weights, w_gate_up, gate_up_scales, w_down, down_scales):
    row_limit = CAP * N_NODE * N_LOCAL
    row_ids = jnp.arange(ROWS, dtype=jnp.int32)
    gate_values = gate_weights.astype(jnp.float32)

    def group_step(combined_sum, group_idx):
        def expert_step(running, member_idx):
            expert_idx = group_idx * EXP_GROUP + member_idx
            hit_mask = expert_ids == expert_idx
            route_gate = jnp.sum(jnp.where(hit_mask, gate_values, jnp.float32(0.0)), axis=1)
            chosen = jnp.any(hit_mask, axis=1)
            row_order = jnp.argsort(jnp.where(chosen, 0, 1).astype(jnp.int32) * ROWS + row_ids)
            row_index = row_order[:row_limit].astype(jnp.int32)
            operand = tokens[row_index]

            def slice_step(total, slice_idx):
                which = expert_idx * SHARD + slice_idx
                outputs = expert_apply(operand, w_gate_up[which], gate_up_scales[which], w_down[which], down_scales[which])
                return total + outputs.astype(jnp.float32), None

            expert_out, unused = lax.scan(slice_step, jnp.zeros((row_limit, D), jnp.float32), jnp.arange(SHARD, dtype=jnp.int32))
            running = running.at[row_index].add(route_gate[row_index][:, None] * expert_out)
            return running, None

        partial_sum, unused = lax.scan(expert_step, jnp.zeros((ROWS, D), jnp.float32), jnp.arange(EXP_GROUP, dtype=jnp.int32))
        rounded = lax.optimization_barrier(partial_sum.astype(jnp.bfloat16))
        return combined_sum + rounded.astype(jnp.float32), None

    combined_sum, unused = lax.scan(group_step, jnp.zeros((ROWS, D), jnp.float32), jnp.arange(N_NODE, dtype=jnp.int32))
    return combined_sum.astype(jnp.bfloat16)
```

```python
import functools

import jax
import jax.numpy as jnp
from jax import lax
from jax.experimental import pallas as pl
from jax.experimental.pallas import tpu as pltpu
from jax.sharding import PartitionSpec as P

EXP_GROUP = 4
LANES = 128
BLOCK = 128
VMEM = pl.BlockSpec(memory_space=pltpu.VMEM)
SMEM = pl.BlockSpec(memory_space=pltpu.SMEM)


def pack_kernel(tokens_ref, ids_ref, gates_ref, out_ref):
    rows, width = tokens_ref.shape
    out_ref[:, :width] = tokens_ref[...]
    lane = lax.broadcasted_iota(jnp.int32, (rows, LANES), 1)
    ids = ids_ref[...]
    gates = gates_ref[...].astype(jnp.float32)
    route = jnp.zeros((rows, LANES), jnp.float32)
    for k in range(ids.shape[1]):
        route = route + jnp.where(ids[:, k : k + 1] == lane, gates[:, k : k + 1], 0.0)
    out_ref[:, width:] = route.astype(jnp.bfloat16)


def pack_rows(tokens, ids, gates):
    rows, width = tokens.shape
    return pl.pallas_call(
        pack_kernel,
        out_shape=jax.ShapeDtypeStruct((rows, width + LANES), jnp.bfloat16),
        in_specs=[VMEM, VMEM, VMEM],
        out_specs=VMEM,
    )(tokens, ids, gates)


def tile_of(width, most=512):
    tile = most
    while width % tile:
        tile -= BLOCK
    return tile


def expert_kernel(which_ref, rows_ref, up_ref, up_scale_ref, down_ref, down_scale_ref, out_ref, hidden_ref, act_ref):
    count = rows_ref.shape[0]
    depth, pair = up_ref.shape
    half, width = down_ref.shape
    tile = tile_of(pair)

    @pl.loop(0, pair // tile)
    def _(step):
        cols = pl.ds(pl.multiple_of(step * tile, tile), tile)
        total = jnp.zeros((count, tile), jnp.float32)
        for b in range(depth // BLOCK):
            part = jnp.dot(
                rows_ref[:, b * BLOCK : (b + 1) * BLOCK],
                up_ref[b * BLOCK : (b + 1) * BLOCK, cols],
                preferred_element_type=jnp.float32,
            )
            total = total + part * up_scale_ref[b : b + 1, cols]
        hidden_ref[:, cols] = total

    gate = hidden_ref[:, :half]
    act_ref[...] = (gate / (1.0 + jnp.exp(-gate)) * hidden_ref[:, half:]).astype(jnp.bfloat16)
    route = rows_ref[:, depth:].astype(jnp.float32)
    lane = lax.broadcasted_iota(jnp.int32, route.shape, 1)
    mine = jnp.sum(jnp.where(lane == which_ref[0], route, 0.0), axis=1, keepdims=True)
    tile_out = tile_of(width)

    @pl.loop(0, width // tile_out)
    def _(step):
        cols = pl.ds(pl.multiple_of(step * tile_out, tile_out), tile_out)
        total = jnp.zeros((count, tile_out), jnp.float32)
        for b in range(half // BLOCK):
            part = jnp.dot(
                act_ref[:, b * BLOCK : (b + 1) * BLOCK],
                down_ref[b * BLOCK : (b + 1) * BLOCK, cols],
                preferred_element_type=jnp.float32,
            )
            total = total + part * down_scale_ref[b : b + 1, cols]
        out_ref[:, cols] = jnp.where(mine > 0, total * mine, 0.0).astype(jnp.bfloat16)


def expert_apply(which, rows, up, up_scale, down, down_scale):
    count = rows.shape[0]
    half, width = down.shape
    moved = (up.size + down.size) * 2
    return pl.pallas_call(
        expert_kernel,
        out_shape=jax.ShapeDtypeStruct((count, width), jnp.bfloat16),
        in_specs=[SMEM] + [VMEM] * 5,
        out_specs=VMEM,
        scratch_shapes=[
            pltpu.VMEM((count, 2 * half), jnp.float32),
            pltpu.VMEM((count, half), jnp.bfloat16),
        ],
        compiler_params=pltpu.CompilerParams(vmem_limit_bytes=14 << 20),
        cost_estimate=pl.CostEstimate(
            flops=2 * count * (up.size + down.size), bytes_accessed=moved, transcendentals=count * half
        ),
    )(which, rows, up, up_scale, down, down_scale)


def xor_pairs(size, step):
    return [(i, i ^ step) for i in range(size)]


def shards(tokens, expert_ids, gate_weights, w_gate_up, gate_up_scales, w_down, down_scales):
    node_count = lax.axis_size("node")
    local_count = lax.axis_size("local")
    chip_count = local_count // 2
    row_count, width = tokens.shape
    slice_count = local_count // EXP_GROUP
    over_node = lambda v, d: lax.ppermute(v, "node", xor_pairs(node_count, d))
    over_local = lambda v, d: lax.ppermute(v, "local", xor_pairs(local_count, d))
    add = lambda a, b: a.astype(jnp.float32) + b.astype(jnp.float32)

    which = (lax.axis_index("node") * EXP_GROUP + lax.axis_index("local") // slice_count).astype(jnp.int32)[None]
    up = pltpu.with_memory_space_constraint(w_gate_up[0], pltpu.VMEM)
    down = pltpu.with_memory_space_constraint(w_down[0], pltpu.VMEM)
    up_scale = jnp.repeat(gate_up_scales[0], BLOCK, axis=1)
    down_scale = jnp.repeat(down_scales[0], BLOCK, axis=1)

    packed = pack_rows(tokens, expert_ids, gate_weights)
    from_node = [packed] + [None] * (node_count - 1)
    for dz in range(node_count - 1, 0, -1):
        from_node[dz] = over_node(packed, dz)
    half_nodes = node_count // 2
    groups = [[node_count - 1 - i for i in range(half_nodes // 2)] + list(range(half_nodes // 2)), []]
    groups[1] = [dz for dz in range(node_count - 1, -1, -1) if dz not in groups[0]]

    returned = []
    for group in groups:
        same_core = []
        for dz in group:
            same_core.append(from_node[dz])
            for dx in range(1, chip_count):
                same_core.append(over_local(from_node[dz], 2 * dx))
        same_core = jnp.concatenate(same_core, axis=0)
        rows = jnp.concatenate([same_core, over_local(same_core, 1)], axis=0)
        outputs = expert_apply(which, rows, up, up_scale, down, down_scale)
        outputs = outputs.reshape(2, len(group), chip_count, row_count, width)
        for i, dz in enumerate(group):
            chip_sum = add(outputs[0, i], over_local(outputs[1, i], 1)).astype(jnp.bfloat16)
            partial = chip_sum[0].astype(jnp.float32)
            for dx in range(1, chip_count):
                partial = partial + over_local(chip_sum[dx], 2 * dx).astype(jnp.float32)
            partial = partial.astype(jnp.bfloat16)
            returned.append(over_node(partial, dz) if dz else partial)
    combined = functools.reduce(jnp.add, [v.astype(jnp.float32) for v in returned])
    return combined.astype(jnp.bfloat16)


def solution(mesh):
    rows = P(("parts", "node", "local"), None)
    held = P(("node", "local"), None, None)
    return jax.shard_map(
        shards,
        mesh=mesh,
        in_specs=(rows, rows, rows, held, held, held, held),
        out_specs=rows,
        check_vma=False,
    )
```

```python
import functools

import jax
import jax.numpy as jnp
from jax import lax
from jax.experimental import pallas as pl
from jax.experimental.pallas import tpu as pltpu
from jax.sharding import PartitionSpec as P

EXP_GROUP = 4
LANES = 128
LOADS = 4
BLOCK = 128
VMEM = pl.BlockSpec(memory_space=pltpu.VMEM)
HBM = pl.BlockSpec(memory_space=pltpu.HBM)


def pack_kernel(tokens_hbm, ids_hbm, gates_hbm, out_ref, ids_ref, gates_ref, sems):
    width = tokens_hbm.shape[1]
    rows = out_ref.shape[0]
    copies = [
        pltpu.make_async_copy(ids_hbm, ids_ref, sems.at[0]),
        pltpu.make_async_copy(gates_hbm, gates_ref, sems.at[1]),
        pltpu.make_async_copy(tokens_hbm, out_ref.at[:, pl.ds(0, width)], sems.at[2]),
    ]
    for copy in copies:
        copy.start()
    copies[0].wait()
    copies[1].wait()
    lane = lax.broadcasted_iota(jnp.int32, (rows, LANES), 1)
    ids = ids_ref[...]
    gates = gates_ref[...].astype(jnp.float32)
    route = jnp.zeros((rows, LANES), jnp.float32)
    for k in range(ids.shape[1]):
        route = route + jnp.where(ids[:, k : k + 1] == lane, gates[:, k : k + 1], 0.0)
    out_ref[:, width:] = route.astype(jnp.bfloat16)
    copies[2].wait()


def pack_rows(tokens, ids, gates):
    rows, width = tokens.shape
    return pl.pallas_call(
        pack_kernel,
        out_shape=pltpu.VMEM((rows, width + LANES), jnp.bfloat16),
        in_specs=[HBM, HBM, HBM],
        out_specs=VMEM,
        scratch_shapes=[
            pltpu.VMEM(ids.shape, ids.dtype),
            pltpu.VMEM(gates.shape, gates.dtype),
            pltpu.SemaphoreType.DMA((3,)),
        ],
        compiler_params=pltpu.CompilerParams(vmem_limit_bytes=2 << 20),
    )(in_hbm(tokens), in_hbm(ids), in_hbm(gates))


def tile_of(width, most=512):
    tile = min(width, most)
    while width % tile:
        tile -= BLOCK
    return tile


def spread(scales, contract, columns):
    blocks = columns // BLOCK
    col = lax.broadcasted_iota(jnp.int32, (blocks, columns), 1) // BLOCK
    row = lax.broadcasted_iota(jnp.int32, (blocks, columns), 0)
    wide = lax.dot_general(
        scales.astype(jnp.bfloat16),
        (col == row).astype(jnp.bfloat16),
        (((contract,), (0,)), ((), ())),
        preferred_element_type=jnp.float32,
    )
    return wide.astype(jnp.bfloat16)


def scales_kernel(up_scale_ref, down_scale_ref, up_wide_ref, down_wide_ref):
    up_wide_ref[...] = spread(up_scale_ref[...], 0, up_wide_ref.shape[1])
    down_wide_ref[...] = spread(down_scale_ref[...], 1, down_wide_ref.shape[1])


def spread_scales(up_scale, down_scale):
    return pl.pallas_call(
        scales_kernel,
        out_shape=[
            pltpu.VMEM((up_scale.shape[1], up_scale.shape[0] * BLOCK), jnp.bfloat16),
            pltpu.VMEM((down_scale.shape[0], down_scale.shape[1] * BLOCK), jnp.bfloat16),
        ],
        in_specs=[VMEM, VMEM],
        out_specs=[VMEM, VMEM],
        compiler_params=pltpu.CompilerParams(vmem_limit_bytes=4 << 20),
    )(up_scale, down_scale)


def load_kernel(start, weights_hbm, out_ref, sem):
    rows, columns = out_ref.shape
    copy = pltpu.make_async_copy(weights_hbm.at[pl.ds(start, rows), pl.ds(0, columns)], out_ref, sem)
    copy.start()
    copy.wait()


def load_rows(weights, start, rows, columns):
    return pl.pallas_call(
        functools.partial(load_kernel, start),
        out_shape=pltpu.VMEM((rows, columns), weights.dtype),
        in_specs=[HBM],
        out_specs=VMEM,
        scratch_shapes=[pltpu.SemaphoreType.DMA],
        compiler_params=pltpu.CompilerParams(vmem_limit_bytes=1 << 20),
        cost_estimate=pl.CostEstimate(flops=0, bytes_accessed=2 * rows * columns, transcendentals=0),
    )(in_hbm(weights))


def scaled(weights, scales):
    rows, columns = weights.shape
    blocks = weights.reshape(rows // BLOCK, BLOCK, columns) * scales[:, None, :]
    return blocks.reshape(rows, columns)


def expert_kernel(slice_count, pieces, rows_ref, *refs):
    gate_refs, refs = refs[:pieces], refs[pieces:]
    (up_scale_ref, down_scale_ref, pair_hbm, down_hbm, out_ref,
     up_ref, down_ref, hidden_ref, act_ref, up_sems, down_sems) = refs
    depth = pair_hbm.shape[0]
    half, width = down_hbm.shape
    tile, tile_out = tile_of(half), tile_of(width, 1024)
    steps, steps_out = half // tile, width // tile_out
    share = -(-steps_out // steps)
    band = depth // pieces

    def up_copy(i):
        return pltpu.make_async_copy(
            pair_hbm.at[:, pl.ds(half + i * tile, tile)], up_ref.at[:, pl.ds(i * tile, tile)], up_sems.at[i]
        )

    def down_copy(i):
        cols = pl.ds(i * tile_out, tile_out)
        return pltpu.make_async_copy(down_hbm.at[:, cols], down_ref.at[:, cols], down_sems.at[i])

    for i in range(steps):
        up_copy(i).start()
    for i in range(steps):
        cols = pl.ds(i * tile, tile)
        total = None
        for p in range(pieces):
            scales = up_scale_ref[p * band // BLOCK : (p + 1) * band // BLOCK, cols]
            part = jnp.dot(
                rows_ref[:, p * band : (p + 1) * band],
                scaled(gate_refs[p][:, cols], scales),
                preferred_element_type=jnp.float32,
            )
            total = part if total is None else total + part
        hidden_ref[:, cols] = total
    for i in range(steps):
        cols = pl.ds(i * tile, tile)
        up_copy(i).wait()
        for k in range(i * share, min(steps_out, i * share + share)):
            down_copy(k).start()
        weights = scaled(up_ref[:, cols], up_scale_ref[:, pl.ds(half + i * tile, tile)])
        other = jnp.dot(rows_ref[:, :depth], weights, preferred_element_type=jnp.float32)
        gate = hidden_ref[:, cols]
        act_ref[:, cols] = (gate / (1.0 + jnp.exp(-gate)) * other).astype(jnp.bfloat16)

    expert = lax.axis_index("node") * EXP_GROUP + lax.axis_index("local") // slice_count
    route = rows_ref[:, depth:].astype(jnp.float32)
    lane = lax.broadcasted_iota(jnp.int32, route.shape, 1)
    mine = jnp.sum(jnp.where(lane == expert, route, 0.0), axis=1, keepdims=True)
    for i in range(steps_out):
        cols = pl.ds(i * tile_out, tile_out)
        down_copy(i).wait()
        weights = scaled(down_ref[:, cols], down_scale_ref[:, cols])
        total = jnp.dot(act_ref[...], weights, preferred_element_type=jnp.float32)
        out_ref[:, cols] = jnp.where(mine > 0, total * mine, 0.0).astype(jnp.bfloat16)


def expert_apply(slice_count, rows, gates, up_scale, down_scale, pair, down):
    count = rows.shape[0]
    half, width = down.shape
    depth = pair.shape[0]
    pieces = len(gates)
    held = 2 * (depth * half + half * width + 3 * count * half)
    return pl.pallas_call(
        functools.partial(expert_kernel, slice_count, pieces),
        out_shape=pltpu.VMEM((count, width), jnp.bfloat16),
        in_specs=[VMEM] * (pieces + 3) + [HBM, HBM],
        out_specs=VMEM,
        scratch_shapes=[
            pltpu.VMEM((depth, half), jnp.bfloat16),
            pltpu.VMEM((half, width), jnp.bfloat16),
            pltpu.VMEM((count, half), jnp.float32),
            pltpu.VMEM((count, half), jnp.bfloat16),
            pltpu.SemaphoreType.DMA((half // tile_of(half),)),
            pltpu.SemaphoreType.DMA((width // tile_of(width, 1024),)),
        ],
        compiler_params=pltpu.CompilerParams(vmem_limit_bytes=held + (5 << 20) + 12 * 1024 * count),
        cost_estimate=pl.CostEstimate(
            flops=2 * count * (pair.size + down.size), bytes_accessed=pair.size + down.size, transcendentals=count * half
        ),
    )(
        in_vmem(rows), *map(in_vmem, gates), in_vmem(up_scale), in_vmem(down_scale), in_hbm(pair), in_hbm(down)
    )


def in_vmem(value):
    return pltpu.with_memory_space_constraint(value, pltpu.VMEM)


def in_hbm(value):
    return pltpu.with_memory_space_constraint(value, pltpu.HBM)


def xor_pairs(size, step):
    return [(i, i ^ step) for i in range(size)]


def shards(tokens, expert_ids, gate_weights, w_gate_up, gate_up_scales, w_down, down_scales):
    node_count = lax.axis_size("node")
    local_count = lax.axis_size("local")
    chip_count = local_count // 2
    row_count, width = tokens.shape
    slice_count = local_count // EXP_GROUP
    over_node = lambda v, d: lax.ppermute(v, "node", xor_pairs(node_count, d))
    over_local = lambda v, d: lax.ppermute(v, "local", xor_pairs(local_count, d))
    add = lambda a, b: a.astype(jnp.float32) + b.astype(jnp.float32)

    pair, down = w_gate_up[0], w_down[0]
    up_scale, down_scale = spread_scales(gate_up_scales[0].T, down_scales[0])
    band = pair.shape[0] // LOADS
    load = lambda source, i: load_rows(source, i * band, band, down.shape[0])
    gates = [load(pair, 0)] + [None] * (LOADS - 1)

    packed = pack_rows(tokens, expert_ids, gate_weights)
    from_node = [packed] + [None] * (node_count - 1)
    for dz in range(node_count - 1, 0, -1):
        from_node[dz] = over_node(packed, dz)
    group = [node_count - 1] + list(range(1, node_count - 1)) + [0]
    same_core = []
    for i, dz in enumerate(group):
        piece = from_node[dz]
        if i == 0:
            piece, gates[0] = lax.optimization_barrier((piece, gates[0]))
        others = [over_local(piece, 2 * dx) for dx in range(1, chip_count)]
        if i < LOADS - 2:
            others, later = lax.optimization_barrier((others, pair))
            gates[i + 1] = load(later, i + 1)
        same_core += [piece, *others]
    gates[-1] = load(pair, LOADS - 1)
    same_core, gates[1:-1] = lax.optimization_barrier((same_core, gates[1:-1]))
    same_core = jnp.concatenate(same_core, axis=0)
    rows = jnp.concatenate([same_core, over_local(same_core, 1)], axis=0)
    outputs = expert_apply(slice_count, rows, gates, up_scale, down_scale, pair, down)
    outputs = outputs.reshape(2, node_count, chip_count, row_count, width)
    returned = []
    for i, dz in enumerate(group):
        chip_sum = add(outputs[0, i], over_local(outputs[1, i], 1)).astype(jnp.bfloat16)
        partial = chip_sum[0].astype(jnp.float32)
        for dx in range(1, chip_count):
            partial = partial + over_local(chip_sum[dx], 2 * dx).astype(jnp.float32)
        partial = partial.astype(jnp.bfloat16)
        returned.append(over_node(partial, dz) if dz else partial)
    combined = functools.reduce(jnp.add, [v.astype(jnp.float32) for v in returned])
    return combined.astype(jnp.bfloat16)


def solution(mesh):
    rows = P(("parts", "node", "local"), None)
    held = P(("node", "local"), None, None)
    return jax.shard_map(
        shards,
        mesh=mesh,
        in_specs=(rows, rows, rows, held, held, held, held),
        out_specs=rows,
        check_vma=False,
    )
```

```python
import functools

import jax
import jax.numpy as jnp
from jax import lax
from jax.experimental import pallas as pl
from jax.experimental.pallas import tpu as pltpu
from jax.sharding import PartitionSpec as P

EXP_GROUP = 4
LANES = 128
BLOCK = 128
VMEM = pl.BlockSpec(memory_space=pltpu.VMEM)
HBM = pl.BlockSpec(memory_space=pltpu.HBM)


def pack_kernel(tokens_hbm, ids_hbm, gates_hbm, out_ref, ids_ref, gates_ref, sems):
    width = tokens_hbm.shape[1]
    rows = out_ref.shape[0]
    copies = [
        pltpu.make_async_copy(ids_hbm, ids_ref, sems.at[0]),
        pltpu.make_async_copy(gates_hbm, gates_ref, sems.at[1]),
        pltpu.make_async_copy(tokens_hbm, out_ref.at[:, pl.ds(0, width)], sems.at[2]),
    ]
    for copy in copies:
        copy.start()
    copies[0].wait()
    copies[1].wait()
    lane = lax.broadcasted_iota(jnp.int32, (rows, LANES), 1)
    ids = ids_ref[...]
    gates = gates_ref[...].astype(jnp.float32)
    route = jnp.zeros((rows, LANES), jnp.float32)
    for k in range(ids.shape[1]):
        route = route + jnp.where(ids[:, k : k + 1] == lane, gates[:, k : k + 1], 0.0)
    out_ref[:, width:] = route.astype(jnp.bfloat16)
    copies[2].wait()


def pack_rows(tokens, ids, gates):
    rows, width = tokens.shape
    return pl.pallas_call(
        pack_kernel,
        out_shape=pltpu.VMEM((rows, width + LANES), jnp.bfloat16),
        in_specs=[HBM, HBM, HBM],
        out_specs=VMEM,
        scratch_shapes=[
            pltpu.VMEM(ids.shape, ids.dtype),
            pltpu.VMEM(gates.shape, gates.dtype),
            pltpu.SemaphoreType.DMA((3,)),
        ],
        compiler_params=pltpu.CompilerParams(vmem_limit_bytes=2 << 20),
    )(in_hbm(tokens), in_hbm(ids), in_hbm(gates))


def tile_of(width, most=512):
    tile = min(width, most)
    while width % tile:
        tile -= BLOCK
    return tile


def spread(scales, contract, columns):
    blocks = columns // BLOCK
    col = lax.broadcasted_iota(jnp.int32, (blocks, columns), 1) // BLOCK
    row = lax.broadcasted_iota(jnp.int32, (blocks, columns), 0)
    wide = lax.dot_general(
        scales.astype(jnp.bfloat16),
        (col == row).astype(jnp.bfloat16),
        (((contract,), (0,)), ((), ())),
        preferred_element_type=jnp.float32,
    )
    return wide.astype(jnp.bfloat16)


def scales_kernel(up_scale_ref, down_scale_ref, up_wide_ref, down_wide_ref):
    up_wide_ref[...] = spread(up_scale_ref[...], 0, up_wide_ref.shape[1])
    down_wide_ref[...] = spread(down_scale_ref[...], 1, down_wide_ref.shape[1])


def spread_scales(up_scale, down_scale):
    return pl.pallas_call(
        scales_kernel,
        out_shape=[
            pltpu.VMEM((up_scale.shape[1], up_scale.shape[0] * BLOCK), jnp.bfloat16),
            pltpu.VMEM((down_scale.shape[0], down_scale.shape[1] * BLOCK), jnp.bfloat16),
        ],
        in_specs=[VMEM, VMEM],
        out_specs=[VMEM, VMEM],
        compiler_params=pltpu.CompilerParams(vmem_limit_bytes=4 << 20),
    )(up_scale, down_scale)


def load_kernel(start, weights_hbm, out_ref, sem):
    rows, columns = out_ref.shape
    copy = pltpu.make_async_copy(weights_hbm.at[pl.ds(start, rows), pl.ds(0, columns)], out_ref, sem)
    copy.start()
    copy.wait()


def load_rows(weights, start, rows, columns):
    return pl.pallas_call(
        functools.partial(load_kernel, start),
        out_shape=pltpu.VMEM((rows, columns), weights.dtype),
        in_specs=[HBM],
        out_specs=VMEM,
        scratch_shapes=[pltpu.SemaphoreType.DMA],
        compiler_params=pltpu.CompilerParams(vmem_limit_bytes=1 << 20),
        cost_estimate=pl.CostEstimate(flops=0, bytes_accessed=2 * rows * columns, transcendentals=0),
    )(in_hbm(weights))


def scaled(weights, scales):
    rows, columns = weights.shape
    blocks = weights.reshape(rows // BLOCK, BLOCK, columns) * scales[:, None, :]
    return blocks.reshape(rows, columns)


def expert_kernel(slice_count, pieces, rows_ref, *refs):
    gate_refs, refs = list(refs[:pieces]), refs[pieces:]
    (up_scale_ref, down_scale_ref, pair_hbm, down_hbm, out_ref,
     last_ref, up_ref, down_ref, hidden_ref, act_ref, last_sem, up_sems, down_sems) = refs
    gate_refs.append(last_ref)
    depth = pair_hbm.shape[0]
    half, width = down_hbm.shape
    tile, tile_out = tile_of(half), tile_of(width, 1024)
    steps, steps_out = half // tile, width // tile_out
    share = -(-steps_out // steps)
    band = last_ref.shape[0]
    starts = [0]
    for gate_ref in gate_refs:
        starts.append(starts[-1] + gate_ref.shape[0])

    def up_copy(i):
        return pltpu.make_async_copy(
            pair_hbm.at[:, pl.ds(half + i * tile, tile)], up_ref.at[:, pl.ds(i * tile, tile)], up_sems.at[i]
        )

    def down_copy(i):
        cols = pl.ds(i * tile_out, tile_out)
        return pltpu.make_async_copy(down_hbm.at[:, cols], down_ref.at[:, cols], down_sems.at[i])

    last_copy = pltpu.make_async_copy(pair_hbm.at[pl.ds(depth - band, band), pl.ds(0, half)], last_ref, last_sem)
    last_copy.start()
    for i in range(steps):
        cols = pl.ds(i * tile, tile)
        total = None
        for p in range(pieces + 1):
            if i == 0 and p == pieces:
                last_copy.wait()
            if p == 1:
                up_copy(i).start()
            first, end = starts[p], starts[p + 1]
            scales = up_scale_ref[first // BLOCK : end // BLOCK, cols]
            part = jnp.dot(
                rows_ref[:, first:end],
                scaled(gate_refs[p][:, cols], scales),
                preferred_element_type=jnp.float32,
            )
            total = part if total is None else total + part
        hidden_ref[:, cols] = total
    for i in range(steps):
        cols = pl.ds(i * tile, tile)
        up_copy(i).wait()
        for k in range(i * share, min(steps_out, i * share + share)):
            down_copy(k).start()
        weights = scaled(up_ref[:, cols], up_scale_ref[:, pl.ds(half + i * tile, tile)])
        other = jnp.dot(rows_ref[:, :depth], weights, preferred_element_type=jnp.float32)
        gate = hidden_ref[:, cols]
        act_ref[:, cols] = (gate / (1.0 + jnp.exp(-gate)) * other).astype(jnp.bfloat16)

    expert = lax.axis_index("node") * EXP_GROUP + lax.axis_index("local") // slice_count
    route = rows_ref[:, depth:].astype(jnp.float32)
    lane = lax.broadcasted_iota(jnp.int32, route.shape, 1)
    mine = jnp.sum(jnp.where(lane == expert, route, 0.0), axis=1, keepdims=True)
    for i in range(steps_out):
        cols = pl.ds(i * tile_out, tile_out)
        down_copy(i).wait()
        weights = scaled(down_ref[:, cols], down_scale_ref[:, cols])
        total = jnp.dot(act_ref[...], weights, preferred_element_type=jnp.float32)
        out_ref[:, cols] = jnp.where(mine > 0, total * mine, 0.0).astype(jnp.bfloat16)


def expert_apply(slice_count, rows, gates, up_scale, down_scale, pair, down):
    count = rows.shape[0]
    half, width = down.shape
    depth = pair.shape[0]
    pieces = len(gates)
    band = depth - sum(g.shape[0] for g in gates)
    held = 2 * (band * half + depth * half + half * width + 3 * count * half)
    return pl.pallas_call(
        functools.partial(expert_kernel, slice_count, pieces),
        out_shape=pltpu.VMEM((count, width), jnp.bfloat16),
        in_specs=[VMEM] * (pieces + 3) + [HBM, HBM],
        out_specs=VMEM,
        scratch_shapes=[
            pltpu.VMEM((band, half), jnp.bfloat16),
            pltpu.VMEM((depth, half), jnp.bfloat16),
            pltpu.VMEM((half, width), jnp.bfloat16),
            pltpu.VMEM((count, half), jnp.float32),
            pltpu.VMEM((count, half), jnp.bfloat16),
            pltpu.SemaphoreType.DMA,
            pltpu.SemaphoreType.DMA((half // tile_of(half),)),
            pltpu.SemaphoreType.DMA((width // tile_of(width, 1024),)),
        ],
        compiler_params=pltpu.CompilerParams(vmem_limit_bytes=held + (5 << 20) + 12 * 1024 * count),
        cost_estimate=pl.CostEstimate(
            flops=2 * count * (pair.size + down.size), bytes_accessed=pair.size + down.size, transcendentals=count * half
        ),
    )(
        in_vmem(rows), *map(in_vmem, gates), in_vmem(up_scale), in_vmem(down_scale), in_hbm(pair), in_hbm(down)
    )


def in_vmem(value):
    return pltpu.with_memory_space_constraint(value, pltpu.VMEM)


def in_hbm(value):
    return pltpu.with_memory_space_constraint(value, pltpu.HBM)


def xor_pairs(size, step):
    return [(i, i ^ step) for i in range(size)]


def shards(tokens, expert_ids, gate_weights, w_gate_up, gate_up_scales, w_down, down_scales):
    node_count = lax.axis_size("node")
    local_count = lax.axis_size("local")
    chip_count = local_count // 2
    row_count, width = tokens.shape
    slice_count = local_count // EXP_GROUP
    over_node = lambda v, d: lax.ppermute(v, "node", xor_pairs(node_count, d))
    over_local = lambda v, d: lax.ppermute(v, "local", xor_pairs(local_count, d))
    add = lambda a, b: a.astype(jnp.float32) + b.astype(jnp.float32)

    pair, down = w_gate_up[0], w_down[0]
    up_scale, down_scale = spread_scales(gate_up_scales[0].T, down_scales[0])
    blocks = pair.shape[0] // BLOCK
    first, second = blocks // 4 * BLOCK, blocks * 3 // 8 * BLOCK

    packed = pack_rows(tokens, expert_ids, gate_weights)
    from_node = [packed] + [None] * (node_count - 1)
    for dz in range(node_count - 1, 0, -1):
        from_node[dz] = over_node(packed, dz)
    group = list(range(node_count - 1, -1, -1))
    over_both = lambda v, dz, dx: lax.ppermute(
        v, ("node", "local"), xor_pairs(node_count * local_count, dz * local_count + 2 * dx)
    )
    over_chips = lambda v: [over_local(v, 2 * dx) for dx in range(1, chip_count)]
    own = over_chips(packed)
    direct = [over_both(packed, 1, dx) for dx in range(1, chip_count)]
    gates = [load_rows(pair, 0, first, down.shape[0])]
    pieces, others = {}, {0: own, 1: direct}
    for dz in group:
        pieces[dz] = from_node[dz]
        if dz == node_count - 1:
            pieces[dz], gates[0] = lax.optimization_barrier((pieces[dz], gates[0]))
        if dz > 1:
            others[dz] = over_chips(pieces[dz])
    others[1], later = lax.optimization_barrier((others[1], pair))
    gates.append(load_rows(later, first, second, down.shape[0]))
    others, gates[1] = lax.optimization_barrier((others, gates[1]))
    same_core = [jnp.concatenate([pieces[dz], *others[dz]], axis=0) for dz in group]
    rows = jnp.concatenate(same_core + [over_local(v, 1) for v in same_core], axis=0)
    outputs = expert_apply(slice_count, rows, gates, up_scale, down_scale, pair, down)
    outputs = outputs.reshape(2, node_count, chip_count, row_count, width)
    returned = []
    for i, dz in enumerate(group):
        chip_sum = add(outputs[0, i], over_local(outputs[1, i], 1)).astype(jnp.bfloat16)
        if dz == 1:
            returned += [over_both(chip_sum[dx], dz, dx) for dx in range(chip_count)]
            continue
        partial = chip_sum[0].astype(jnp.float32)
        for dx in range(1, chip_count):
            partial = partial + over_local(chip_sum[dx], 2 * dx).astype(jnp.float32)
        partial = partial.astype(jnp.bfloat16)
        returned.append(over_node(partial, dz) if dz else partial)
    combined = functools.reduce(jnp.add, [v.astype(jnp.float32) for v in returned])
    return combined.astype(jnp.bfloat16)


def solution(mesh):
    rows = P(("parts", "node", "local"), None)
    held = P(("node", "local"), None, None)
    return jax.shard_map(
        shards,
        mesh=mesh,
        in_specs=(rows, rows, rows, held, held, held, held),
        out_specs=rows,
        check_vma=False,
    )
```

```python
import functools

import jax
import jax.numpy as jnp
from jax import lax
from jax.experimental import pallas as pl
from jax.experimental.pallas import tpu as pltpu
from jax.sharding import PartitionSpec as P

EXP_GROUP = 4
LANES = 128
BLOCK = 128
VMEM = pl.BlockSpec(memory_space=pltpu.VMEM)
HBM = pl.BlockSpec(memory_space=pltpu.HBM)


def pack_kernel(tokens_hbm, ids_hbm, gates_hbm, out_ref, ids_ref, gates_ref, sems):
    width = tokens_hbm.shape[1]
    rows = out_ref.shape[0]
    copies = [
        pltpu.make_async_copy(ids_hbm, ids_ref, sems.at[0]),
        pltpu.make_async_copy(gates_hbm, gates_ref, sems.at[1]),
        pltpu.make_async_copy(tokens_hbm, out_ref.at[:, pl.ds(0, width)], sems.at[2]),
    ]
    for copy in copies:
        copy.start()
    copies[0].wait()
    copies[1].wait()
    lane = lax.broadcasted_iota(jnp.int32, (rows, LANES), 1)
    ids = ids_ref[...]
    gates = gates_ref[...].astype(jnp.float32)
    route = jnp.zeros((rows, LANES), jnp.float32)
    for k in range(ids.shape[1]):
        route = route + jnp.where(ids[:, k : k + 1] == lane, gates[:, k : k + 1], 0.0)
    out_ref[:, width:] = route.astype(jnp.bfloat16)
    copies[2].wait()


def pack_rows(tokens, ids, gates):
    rows, width = tokens.shape
    return pl.pallas_call(
        pack_kernel,
        out_shape=pltpu.VMEM((rows, width + LANES), jnp.bfloat16),
        in_specs=[HBM, HBM, HBM],
        out_specs=VMEM,
        scratch_shapes=[
            pltpu.VMEM(ids.shape, ids.dtype),
            pltpu.VMEM(gates.shape, gates.dtype),
            pltpu.SemaphoreType.DMA((3,)),
        ],
        compiler_params=pltpu.CompilerParams(vmem_limit_bytes=2 << 20),
    )(in_hbm(tokens), in_hbm(ids), in_hbm(gates))


def tile_of(width, most=512):
    tile = min(width, most)
    while width % tile:
        tile -= BLOCK
    return tile


def spread(scales, contract, columns):
    blocks = columns // BLOCK
    col = lax.broadcasted_iota(jnp.int32, (blocks, columns), 1) // BLOCK
    row = lax.broadcasted_iota(jnp.int32, (blocks, columns), 0)
    wide = lax.dot_general(
        scales.astype(jnp.bfloat16),
        (col == row).astype(jnp.bfloat16),
        (((contract,), (0,)), ((), ())),
        preferred_element_type=jnp.float32,
    )
    return wide.astype(jnp.bfloat16)


def scales_kernel(up_scale_ref, down_scale_ref, up_wide_ref, down_wide_ref):
    up_wide_ref[...] = spread(up_scale_ref[...], 0, up_wide_ref.shape[1])
    down_wide_ref[...] = spread(down_scale_ref[...], 1, down_wide_ref.shape[1])


def spread_scales(up_scale, down_scale):
    return pl.pallas_call(
        scales_kernel,
        out_shape=[
            pltpu.VMEM((up_scale.shape[1], up_scale.shape[0] * BLOCK), jnp.bfloat16),
            pltpu.VMEM((down_scale.shape[0], down_scale.shape[1] * BLOCK), jnp.bfloat16),
        ],
        in_specs=[VMEM, VMEM],
        out_specs=[VMEM, VMEM],
        compiler_params=pltpu.CompilerParams(vmem_limit_bytes=4 << 20),
    )(up_scale, down_scale)


def load_kernel(start, weights_hbm, out_ref, sem):
    rows, columns = out_ref.shape
    copy = pltpu.make_async_copy(weights_hbm.at[pl.ds(start, rows), pl.ds(0, columns)], out_ref, sem)
    copy.start()
    copy.wait()


def load_rows(weights, start, rows, columns):
    return pl.pallas_call(
        functools.partial(load_kernel, start),
        out_shape=pltpu.VMEM((rows, columns), weights.dtype),
        in_specs=[HBM],
        out_specs=VMEM,
        scratch_shapes=[pltpu.SemaphoreType.DMA],
        compiler_params=pltpu.CompilerParams(vmem_limit_bytes=1 << 20),
        cost_estimate=pl.CostEstimate(flops=0, bytes_accessed=2 * rows * columns, transcendentals=0),
    )(in_hbm(weights))


def scaled(weights, scales):
    rows, columns = weights.shape
    blocks = weights.reshape(rows // BLOCK, BLOCK, columns) * scales[:, None, :]
    return blocks.reshape(rows, columns)


def expert_kernel(slice_count, pieces, rows_ref, *refs):
    gate_refs, refs = list(refs[:pieces]), refs[pieces:]
    (up_scale_ref, down_scale_ref, pair_hbm, down_hbm, out_ref,
     last_ref, up_ref, down_ref, hidden_ref, act_ref, last_sem, up_sems, down_sems) = refs
    gate_refs.append(last_ref)
    depth = pair_hbm.shape[0]
    half, width = down_hbm.shape
    tile, tile_out = tile_of(half), tile_of(width, 1024)
    steps, steps_out = half // tile, width // tile_out
    share = -(-steps_out // steps)
    band = last_ref.shape[0]
    starts = [0]
    for gate_ref in gate_refs:
        starts.append(starts[-1] + gate_ref.shape[0])

    def up_copy(i):
        return pltpu.make_async_copy(
            pair_hbm.at[:, pl.ds(half + i * tile, tile)], up_ref.at[:, pl.ds(i * tile, tile)], up_sems.at[i]
        )

    def down_copy(i):
        cols = pl.ds(i * tile_out, tile_out)
        return pltpu.make_async_copy(down_hbm.at[:, cols], down_ref.at[:, cols], down_sems.at[i])

    last_copy = pltpu.make_async_copy(pair_hbm.at[pl.ds(depth - band, band), pl.ds(0, half)], last_ref, last_sem)
    last_copy.start()
    for i in range(steps):
        cols = pl.ds(i * tile, tile)
        total = None
        for p in range(pieces + 1):
            if i == 0 and p == pieces:
                last_copy.wait()
            if p == 1:
                up_copy(i).start()
            first, end = starts[p], starts[p + 1]
            scales = up_scale_ref[first // BLOCK : end // BLOCK, cols]
            part = jnp.dot(
                rows_ref[:, first:end],
                scaled(gate_refs[p][:, cols], scales),
                preferred_element_type=jnp.float32,
            )
            total = part if total is None else total + part
        hidden_ref[:, cols] = total
    for i in range(steps):
        cols = pl.ds(i * tile, tile)
        up_copy(i).wait()
        for k in range(i * share, min(steps_out, i * share + share)):
            down_copy(k).start()
        weights = scaled(up_ref[:, cols], up_scale_ref[:, pl.ds(half + i * tile, tile)])
        other = jnp.dot(rows_ref[:, :depth], weights, preferred_element_type=jnp.float32)
        gate = hidden_ref[:, cols]
        act_ref[:, cols] = (gate / (1.0 + jnp.exp(-gate)) * other).astype(jnp.bfloat16)

    expert = lax.axis_index("node") * EXP_GROUP + lax.axis_index("local") // slice_count
    route = rows_ref[:, depth:].astype(jnp.float32)
    lane = lax.broadcasted_iota(jnp.int32, route.shape, 1)
    mine = jnp.sum(jnp.where(lane == expert, route, 0.0), axis=1, keepdims=True)
    for i in range(steps_out):
        cols = pl.ds(i * tile_out, tile_out)
        down_copy(i).wait()
        weights = scaled(down_ref[:, cols], down_scale_ref[:, cols])
        total = jnp.dot(act_ref[...], weights, preferred_element_type=jnp.float32)
        out_ref[:, cols] = jnp.where(mine > 0, total * mine, 0.0).astype(jnp.bfloat16)


def expert_apply(slice_count, rows, gates, up_scale, down_scale, pair, down):
    count = rows.shape[0]
    half, width = down.shape
    depth = pair.shape[0]
    pieces = len(gates)
    band = depth - sum(g.shape[0] for g in gates)
    held = 2 * (band * half + depth * half + half * width + 3 * count * half)
    return pl.pallas_call(
        functools.partial(expert_kernel, slice_count, pieces),
        out_shape=pltpu.VMEM((count, width), jnp.bfloat16),
        in_specs=[VMEM] * (pieces + 3) + [HBM, HBM],
        out_specs=VMEM,
        scratch_shapes=[
            pltpu.VMEM((band, half), jnp.bfloat16),
            pltpu.VMEM((depth, half), jnp.bfloat16),
            pltpu.VMEM((half, width), jnp.bfloat16),
            pltpu.VMEM((count, half), jnp.float32),
            pltpu.VMEM((count, half), jnp.bfloat16),
            pltpu.SemaphoreType.DMA,
            pltpu.SemaphoreType.DMA((half // tile_of(half),)),
            pltpu.SemaphoreType.DMA((width // tile_of(width, 1024),)),
        ],
        compiler_params=pltpu.CompilerParams(vmem_limit_bytes=held + (5 << 20) + 12 * 1024 * count),
        cost_estimate=pl.CostEstimate(
            flops=2 * count * (pair.size + down.size), bytes_accessed=pair.size + down.size, transcendentals=count * half
        ),
    )(
        in_vmem(rows), *map(in_vmem, gates), in_vmem(up_scale), in_vmem(down_scale), in_hbm(pair), in_hbm(down)
    )


def in_vmem(value):
    return pltpu.with_memory_space_constraint(value, pltpu.VMEM)


def in_hbm(value):
    return pltpu.with_memory_space_constraint(value, pltpu.HBM)


def xor_pairs(size, step):
    return [(i, i ^ step) for i in range(size)]


def shards(tokens, expert_ids, gate_weights, w_gate_up, gate_up_scales, w_down, down_scales):
    node_count = lax.axis_size("node")
    local_count = lax.axis_size("local")
    chip_count = local_count // 2
    row_count, width = tokens.shape
    slice_count = local_count // EXP_GROUP
    over_node = lambda v, d: lax.ppermute(v, "node", xor_pairs(node_count, d))
    over_local = lambda v, d: lax.ppermute(v, "local", xor_pairs(local_count, d))
    add = lambda a, b: a.astype(jnp.float32) + b.astype(jnp.float32)

    pair, down = w_gate_up[0], w_down[0]
    up_scale, down_scale = spread_scales(gate_up_scales[0].T, down_scales[0])
    blocks = pair.shape[0] // BLOCK
    first, second = blocks * 3 // 8 * BLOCK, blocks // 2 * BLOCK

    packed = pack_rows(tokens, expert_ids, gate_weights)
    from_node = [packed] + [None] * (node_count - 1)
    for dz in range(node_count - 1, 0, -1):
        from_node[dz] = over_node(packed, dz)
    group = list(range(node_count - 1, -1, -1))
    over_both = lambda v, dz, dx: lax.ppermute(
        v, ("node", "local"), xor_pairs(node_count * local_count, dz * local_count + 2 * dx)
    )
    over_chips = lambda v: [over_local(v, 2 * dx) for dx in range(1, chip_count)]
    own = over_chips(packed)
    direct = [over_both(packed, 1, dx) for dx in range(1, chip_count)]
    gates = [load_rows(pair, 0, first, down.shape[0])]
    pieces, others = {}, {0: own, 1: direct}
    for dz in group:
        pieces[dz] = from_node[dz]
        if dz == node_count - 1:
            pieces[dz], gates[0] = lax.optimization_barrier((pieces[dz], gates[0]))
        if dz > 1:
            others[dz] = over_chips(pieces[dz])
    others[1], later = lax.optimization_barrier((others[1], pair))
    gates.append(load_rows(later, first, second, down.shape[0]))
    others, gates[1] = lax.optimization_barrier((others, gates[1]))
    same_core = [jnp.concatenate([pieces[dz], *others[dz]], axis=0) for dz in group]
    rows = jnp.concatenate(same_core + [over_local(v, 1) for v in same_core], axis=0)
    outputs = expert_apply(slice_count, rows, gates, up_scale, down_scale, pair, down)
    outputs = outputs.reshape(2, node_count, chip_count, row_count, width)
    sums = {}
    for i, dz in enumerate(group):
        sums[dz] = add(outputs[0, i], over_local(outputs[1, i], 1)).astype(jnp.bfloat16)

    def group_sum(first, others):
        total = first.astype(jnp.float32)
        for other in others:
            total = total + other.astype(jnp.float32)
        return total.astype(jnp.bfloat16)

    over_pieces = lambda v: [over_local(v[dx], 2 * dx) for dx in range(1, chip_count)]
    far = range(node_count - 1, 1, -1)
    arrived = {dz: over_pieces(sums[dz]) for dz in far}
    returned = [over_node(group_sum(sums[dz][0], arrived[dz]), dz) for dz in far]
    returned += [over_both(sums[1][dx], 1, dx) for dx in range(chip_count)]
    returned.append(group_sum(sums[0][0], over_pieces(sums[0])))
    combined = functools.reduce(jnp.add, [v.astype(jnp.float32) for v in returned])
    return combined.astype(jnp.bfloat16)


def solution(mesh):
    rows = P(("parts", "node", "local"), None)
    held = P(("node", "local"), None, None)
    return jax.shard_map(
        shards,
        mesh=mesh,
        in_specs=(rows, rows, rows, held, held, held, held),
        out_specs=rows,
        check_vma=False,
    )
```

```python
import functools

import jax
import jax.numpy as jnp
from jax import lax
from jax.experimental import pallas as pl
from jax.experimental.pallas import tpu as pltpu
from jax.sharding import PartitionSpec as P

EXP_GROUP = 4
LANES = 128
BLOCK = 128
VMEM = pl.BlockSpec(memory_space=pltpu.VMEM)
HBM = pl.BlockSpec(memory_space=pltpu.HBM)


def pack_kernel(tokens_hbm, ids_hbm, gates_hbm, out_ref, ids_ref, gates_ref, sems):
    width = tokens_hbm.shape[1]
    rows = out_ref.shape[0]
    copies = [
        pltpu.make_async_copy(ids_hbm, ids_ref, sems.at[0]),
        pltpu.make_async_copy(gates_hbm, gates_ref, sems.at[1]),
        pltpu.make_async_copy(tokens_hbm, out_ref.at[:, pl.ds(0, width)], sems.at[2]),
    ]
    for copy in copies:
        copy.start()
    copies[0].wait()
    copies[1].wait()
    lane = lax.broadcasted_iota(jnp.int32, (rows, LANES), 1)
    ids = ids_ref[...]
    gates = gates_ref[...].astype(jnp.float32)
    route = jnp.zeros((rows, LANES), jnp.float32)
    for k in range(ids.shape[1]):
        route = route + jnp.where(ids[:, k : k + 1] == lane, gates[:, k : k + 1], 0.0)
    out_ref[:, width:] = route.astype(jnp.bfloat16)
    copies[2].wait()


def pack_rows(tokens, ids, gates):
    rows, width = tokens.shape
    return pl.pallas_call(
        pack_kernel,
        out_shape=pltpu.VMEM((rows, width + LANES), jnp.bfloat16),
        in_specs=[HBM, HBM, HBM],
        out_specs=VMEM,
        scratch_shapes=[
            pltpu.VMEM(ids.shape, ids.dtype),
            pltpu.VMEM(gates.shape, gates.dtype),
            pltpu.SemaphoreType.DMA((3,)),
        ],
        compiler_params=pltpu.CompilerParams(vmem_limit_bytes=2 << 20),
    )(in_hbm(tokens), in_hbm(ids), in_hbm(gates))


def tile_of(width, most=512):
    tile = min(width, most)
    while width % tile:
        tile -= BLOCK
    return tile


def spread(scales, contract, columns):
    blocks = columns // BLOCK
    col = lax.broadcasted_iota(jnp.int32, (blocks, columns), 1) // BLOCK
    row = lax.broadcasted_iota(jnp.int32, (blocks, columns), 0)
    wide = lax.dot_general(
        scales.astype(jnp.bfloat16),
        (col == row).astype(jnp.bfloat16),
        (((contract,), (0,)), ((), ())),
        preferred_element_type=jnp.float32,
    )
    return wide.astype(jnp.bfloat16)


def scales_kernel(up_scale_ref, down_scale_ref, up_wide_ref, down_wide_ref):
    up_wide_ref[...] = spread(up_scale_ref[...], 0, up_wide_ref.shape[1])
    down_wide_ref[...] = spread(down_scale_ref[...], 1, down_wide_ref.shape[1])


def spread_scales(up_scale, down_scale):
    return pl.pallas_call(
        scales_kernel,
        out_shape=[
            pltpu.VMEM((up_scale.shape[1], up_scale.shape[0] * BLOCK), jnp.bfloat16),
            pltpu.VMEM((down_scale.shape[0], down_scale.shape[1] * BLOCK), jnp.bfloat16),
        ],
        in_specs=[VMEM, VMEM],
        out_specs=[VMEM, VMEM],
        compiler_params=pltpu.CompilerParams(vmem_limit_bytes=4 << 20),
    )(up_scale, down_scale)


def load_kernel(start, weights_hbm, out_ref, sem):
    rows, columns = out_ref.shape
    copy = pltpu.make_async_copy(weights_hbm.at[pl.ds(start, rows), pl.ds(0, columns)], out_ref, sem)
    copy.start()
    copy.wait()


def load_rows(weights, start, rows, columns):
    return pl.pallas_call(
        functools.partial(load_kernel, start),
        out_shape=pltpu.VMEM((rows, columns), weights.dtype),
        in_specs=[HBM],
        out_specs=VMEM,
        scratch_shapes=[pltpu.SemaphoreType.DMA],
        compiler_params=pltpu.CompilerParams(vmem_limit_bytes=1 << 20),
        cost_estimate=pl.CostEstimate(flops=0, bytes_accessed=2 * rows * columns, transcendentals=0),
    )(in_hbm(weights))


def scaled(weights, scales):
    rows, columns = weights.shape
    blocks = weights.reshape(rows // BLOCK, BLOCK, columns) * scales[:, None, :]
    return blocks.reshape(rows, columns)


def expert_kernel(slice_count, pieces, rows_ref, *refs):
    gate_refs, refs = list(refs[:pieces]), refs[pieces:]
    (up_scale_ref, down_scale_ref, pair_hbm, down_hbm, out_ref,
     last_ref, up_ref, down_ref, hidden_ref, act_ref, last_sem, up_sems, down_sems) = refs
    gate_refs.append(last_ref)
    depth = pair_hbm.shape[0]
    half, width = down_hbm.shape
    tile, tile_out = tile_of(half), tile_of(width, 1024)
    steps, steps_out = half // tile, width // tile_out
    share = -(-steps_out // steps)
    band = last_ref.shape[0]
    starts = [0]
    for gate_ref in gate_refs:
        starts.append(starts[-1] + gate_ref.shape[0])

    def up_copy(i):
        return pltpu.make_async_copy(
            pair_hbm.at[:, pl.ds(half + i * tile, tile)], up_ref.at[:, pl.ds(i * tile, tile)], up_sems.at[i]
        )

    def down_copy(i):
        cols = pl.ds(i * tile_out, tile_out)
        return pltpu.make_async_copy(down_hbm.at[:, cols], down_ref.at[:, cols], down_sems.at[i])

    last_copy = pltpu.make_async_copy(pair_hbm.at[pl.ds(depth - band, band), pl.ds(0, half)], last_ref, last_sem)
    last_copy.start()
    for i in range(steps):
        cols = pl.ds(i * tile, tile)
        total = None
        for p in range(pieces + 1):
            if i == 0 and p == pieces:
                last_copy.wait()
            if p == 1:
                up_copy(i).start()
            first, end = starts[p], starts[p + 1]
            scales = up_scale_ref[first // BLOCK : end // BLOCK, cols]
            part = jnp.dot(
                rows_ref[:, first:end],
                scaled(gate_refs[p][:, cols], scales),
                preferred_element_type=jnp.float32,
            )
            total = part if total is None else total + part
        hidden_ref[:, cols] = total
    for i in range(steps):
        cols = pl.ds(i * tile, tile)
        up_copy(i).wait()
        for k in range(i * share, min(steps_out, i * share + share)):
            down_copy(k).start()
        weights = scaled(up_ref[:, cols], up_scale_ref[:, pl.ds(half + i * tile, tile)])
        other = jnp.dot(rows_ref[:, :depth], weights, preferred_element_type=jnp.float32)
        gate = hidden_ref[:, cols]
        act_ref[:, cols] = (gate / (1.0 + jnp.exp(-gate)) * other).astype(jnp.bfloat16)

    expert = lax.axis_index("node") * EXP_GROUP + lax.axis_index("local") // slice_count
    route = rows_ref[:, depth:].astype(jnp.float32)
    lane = lax.broadcasted_iota(jnp.int32, route.shape, 1)
    mine = jnp.sum(jnp.where(lane == expert, route, 0.0), axis=1, keepdims=True)
    for i in range(steps_out):
        cols = pl.ds(i * tile_out, tile_out)
        down_copy(i).wait()
        weights = scaled(down_ref[:, cols], down_scale_ref[:, cols])
        total = jnp.dot(act_ref[...], weights, preferred_element_type=jnp.float32)
        out_ref[:, cols] = jnp.where(mine > 0, total * mine, 0.0).astype(jnp.bfloat16)


def expert_apply(slice_count, rows, gates, up_scale, down_scale, pair, down):
    count = rows.shape[0]
    half, width = down.shape
    depth = pair.shape[0]
    pieces = len(gates)
    band = depth - sum(g.shape[0] for g in gates)
    held = 2 * (band * half + depth * half + half * width + 3 * count * half)
    return pl.pallas_call(
        functools.partial(expert_kernel, slice_count, pieces),
        out_shape=pltpu.VMEM((count, width), jnp.bfloat16),
        in_specs=[VMEM] * (pieces + 3) + [HBM, HBM],
        out_specs=VMEM,
        scratch_shapes=[
            pltpu.VMEM((band, half), jnp.bfloat16),
            pltpu.VMEM((depth, half), jnp.bfloat16),
            pltpu.VMEM((half, width), jnp.bfloat16),
            pltpu.VMEM((count, half), jnp.float32),
            pltpu.VMEM((count, half), jnp.bfloat16),
            pltpu.SemaphoreType.DMA,
            pltpu.SemaphoreType.DMA((half // tile_of(half),)),
            pltpu.SemaphoreType.DMA((width // tile_of(width, 1024),)),
        ],
        compiler_params=pltpu.CompilerParams(vmem_limit_bytes=held + (5 << 20) + 12 * 1024 * count),
        cost_estimate=pl.CostEstimate(
            flops=2 * count * (pair.size + down.size), bytes_accessed=pair.size + down.size, transcendentals=count * half
        ),
    )(
        in_vmem(rows), *map(in_vmem, gates), in_vmem(up_scale), in_vmem(down_scale), in_hbm(pair), in_hbm(down)
    )


def in_vmem(value):
    return pltpu.with_memory_space_constraint(value, pltpu.VMEM)


def in_hbm(value):
    return pltpu.with_memory_space_constraint(value, pltpu.HBM)


def xor_pairs(size, step):
    return [(i, i ^ step) for i in range(size)]


def shards(tokens, expert_ids, gate_weights, w_gate_up, gate_up_scales, w_down, down_scales):
    node_count = lax.axis_size("node")
    local_count = lax.axis_size("local")
    chip_count = local_count // 2
    row_count, width = tokens.shape
    slice_count = local_count // EXP_GROUP
    over_node = lambda v, d: lax.ppermute(v, "node", xor_pairs(node_count, d))
    over_local = lambda v, d: lax.ppermute(v, "local", xor_pairs(local_count, d))
    add = lambda a, b: a.astype(jnp.float32) + b.astype(jnp.float32)

    pair, down = w_gate_up[0], w_down[0]
    up_scale, down_scale = spread_scales(gate_up_scales[0].T, down_scales[0])
    blocks = pair.shape[0] // BLOCK
    first, second = blocks * 3 // 8 * BLOCK, blocks // 2 * BLOCK

    packed = pack_rows(tokens, expert_ids, gate_weights)
    from_node = [packed] + [None] * (node_count - 1)
    for dz in range(node_count - 1, 0, -1):
        from_node[dz] = over_node(packed, dz)
    group = list(range(node_count - 1, -1, -1))
    over_both = lambda v, dz, dx: lax.ppermute(
        v, ("node", "local"), xor_pairs(node_count * local_count, dz * local_count + 2 * dx)
    )
    over_chips = lambda v: [over_local(v, 2 * dx) for dx in range(1, chip_count)]
    own = over_chips(packed)
    direct = [over_both(packed, 1, dx) for dx in range(1, chip_count)]
    gates = [load_rows(pair, 0, first, down.shape[0])]
    pieces, others = {}, {0: own, 1: direct}
    for dz in group:
        pieces[dz] = from_node[dz]
        if dz == node_count - 1:
            pieces[dz], gates[0] = lax.optimization_barrier((pieces[dz], gates[0]))
        if dz > 1:
            others[dz] = over_chips(pieces[dz])
    others[1], later = lax.optimization_barrier((others[1], pair))
    gates.append(load_rows(later, first, second, down.shape[0]))
    others, gates[1] = lax.optimization_barrier((others, gates[1]))
    same_core = [jnp.concatenate([pieces[dz], *others[dz]], axis=0) for dz in group]
    rows = jnp.concatenate(same_core + [over_local(v, 1) for v in same_core], axis=0)
    outputs = expert_apply(slice_count, rows, gates, up_scale, down_scale, pair, down)
    outputs = outputs.reshape(2, node_count, chip_count, row_count, width)
    sums = {}
    for i, dz in enumerate(group):
        sums[dz] = add(outputs[0, i], over_local(outputs[1, i], 1)).astype(jnp.bfloat16)

    def group_sum(first, others):
        total = first.astype(jnp.float32)
        for other in others:
            total = total + other.astype(jnp.float32)
        return total.astype(jnp.bfloat16)

    over_pieces = lambda v: [over_local(v[dx], 2 * dx) for dx in range(1, chip_count)]
    far = range(2, node_count)
    arrived = {dz: over_pieces(sums[dz]) for dz in far}
    returned = [over_node(group_sum(sums[dz][0], arrived[dz]), dz) for dz in far]
    returned += [over_both(sums[1][dx], 1, dx) for dx in range(chip_count)]
    returned.append(group_sum(sums[0][0], over_pieces(sums[0])))
    combined = functools.reduce(jnp.add, [v.astype(jnp.float32) for v in returned])
    return combined.astype(jnp.bfloat16)


def solution(mesh):
    rows = P(("parts", "node", "local"), None)
    held = P(("node", "local"), None, None)
    return jax.shard_map(
        shards,
        mesh=mesh,
        in_specs=(rows, rows, rows, held, held, held, held),
        out_specs=rows,
        check_vma=False,
    )
```
